256 devices in a mesh: lon: 32 (over x_hi, z, core), lat: 8 (over y, x_lo).
Axes of the slice: x: 4 (x_hi: 2, x_lo: 2; x = x_hi * 2 + x_lo), y: 4, z: 8, core: 2. Of those that a mesh axis runs over, the one named last changes fastest.
Arguments:
- latent_field: bfloat16 [4, 96, 768, 512], P(None, 'lat', 'lon'), may hold values from -48 to 48, as said below
- gain_one: float32 [512], replicated, may hold values from 0.1 to 1.9
- qkv_one: bfloat16 [512, 1536], P('lon'), may hold values from -0.25 to 0.25
- proj_one: bfloat16 [512, 512], P('lon'), may hold values from -0.25 to 0.25
- merge_weight: bfloat16 [2048, 1024], P('lon'), may hold values from -0.125 to 0.125
- gain_two: float32 [1024], replicated, may hold values from 0.1 to 1.9
- qkv_two: bfloat16 [1024, 3072], P('lon'), may hold values from -0.1875 to 0.1875
- proj_two: bfloat16 [1024, 1024], P('lon'), may hold values from -0.1875 to 0.1875
- decode_up: bfloat16 [1024, 512], P('lon'), may hold values from -0.15625 to 0.15625
- decode_skip: bfloat16 [512, 512], P('lon'), may hold values from -0.15625 to 0.15625
Outputs:
- decoded: bfloat16 [4, 96, 768, 512], P(None, 'lat', 'lon')
The draws below stay inside these ranges and needn't reach their ends.
Inputs may be any that keep to these rules, and one draw needn't show every extreme that they name: `latent_field`: activations of the first level.
All inputs are finite; a program needn't handle non-finite values.
Results may differ from the reference program's by a relative error of at most 0.02.
Values may be sent and summed in bfloat16 or wider, within the bound.
A program may use at most 128 MiB of HBM per device.

```python
import jax
import jax.numpy as jnp
from jax import lax

D1 = 512
D2 = 1024
HEADS_ONE = 8
HEADS_TWO = 16
LEVELS = 4
WIN_LEV = 2
WIN_LAT = 6
WIN_LON = 12
NLAT = 96
NLON = 768


def draw_latent_field(key, part):
    key = jax.random.fold_in(key, 11)
    shape = (LEVELS, NLAT, NLON, D1)
    return jax.random.truncated_normal(key, -6.0, 6.0, shape, jnp.float32).astype(jnp.bfloat16)


def steps_of(stream_key, extent, shards, smallest, largest):
    loudness, own = 1.0, jax.random.fold_in(stream_key, 6)
    for position, parts in shards:
        steps = jnp.exp(jax.random.uniform(jax.random.fold_in(own, position), (parts,), jnp.float32, smallest / len(shards), largest / len(shards)))
        loudness = loudness * jnp.repeat(steps, extent[position] // parts).reshape([-1 if axis == position else 1 for axis in range(len(extent))])
    return loudness


def centred(rng, extent, scale, most, cuts=(), kind=jnp.bfloat16):
    level = steps_of(rng, extent, cuts, -0.22, 0.18) if cuts else 1.0
    array = jax.random.normal(rng, extent, jnp.float32) * scale * level
    return jnp.minimum(jnp.maximum(array, -most), most).astype(kind)


def setup_inputs(seed: int = 0) -> dict:
    splits = jax.random.split(jax.random.key(seed), 11)
    latent_field = draw_latent_field(jax.random.fold_in(splits[10], 71), 0)
    gain_one = jnp.clip(1.0 + 0.18 * jax.random.normal(splits[1], (D1,), jnp.float32), 0.1, 1.9)
    qkv_one = centred(splits[2], (D1, 3 * D1), D1 ** -0.5, 0.25, ((0, 32),))
    proj_one = centred(splits[3], (D1, D1), D1 ** -0.5, 0.25, ((0, 32),))
    merge_weight = centred(splits[4], (4 * D1, D2), (4 * D1) ** -0.5, 0.125, ((0, 32),))
    gain_two = jnp.clip(1.0 + 0.18 * jax.random.normal(splits[5], (D2,), jnp.float32), 0.1, 1.9)
    qkv_two = centred(splits[6], (D2, 3 * D2), D2 ** -0.5, 0.1875, ((0, 32),))
    proj_two = centred(splits[7], (D2, D2), D2 ** -0.5, 0.1875, ((0, 32),))
    decode_up = centred(splits[8], (D2, D1), (D1 + D2) ** -0.5, 0.15625, ((0, 32),))
    decode_skip = centred(splits[9], (D1, D1), (D1 + D2) ** -0.5, 0.15625, ((0, 32),))
    return {"latent_field": latent_field, "gain_one": gain_one, "qkv_one": qkv_one, "proj_one": proj_one, "merge_weight": merge_weight, "gain_two": gain_two, "qkv_two": qkv_two, "proj_two": proj_two, "decode_up": decode_up, "decode_skip": decode_skip}


def window_tiles(field, lat_win, lon_win):
    levels, height, width, feats = field.shape
    groups = levels // WIN_LEV
    tiles = field.reshape(groups, WIN_LEV, height // lat_win, lat_win, width // lon_win, lon_win, feats)
    tiles = tiles.transpose(2, 0, 4, 1, 3, 5, 6)
    return tiles.reshape(height // lat_win, groups * (width // lon_win), WIN_LEV * lat_win * lon_win, feats)

def tiles_field(tiles, levels, lat_win, lon_win):
    rows_win, many_win, count, feats = tiles.shape
    groups = levels // WIN_LEV
    cols_win = many_win // groups
    field = tiles.reshape(rows_win, groups, cols_win, WIN_LEV, lat_win, lon_win, feats)
    field = field.transpose(1, 3, 0, 4, 2, 5, 6)
    return field.reshape(levels, rows_win * lat_win, cols_win * lon_win, feats)

def layer_norm(values, gain):
    center = values - lax.optimization_barrier(jnp.mean(values, axis=-1, keepdims=True))
    spread = lax.optimization_barrier(jnp.mean(center * center, axis=-1, keepdims=True))
    return center * lax.rsqrt(spread + 1e-05) * gain.astype(jnp.float32)

def attend(qkv, region, heads):
    windows, count, triple = qkv.shape
    feats = triple // 3
    head_dim = feats // heads
    query = qkv[..., :feats].reshape(windows, count, heads, head_dim).astype(jnp.float32)
    keys = qkv[..., feats:2 * feats].reshape(windows, count, heads, head_dim).astype(jnp.float32)
    values = qkv[..., 2 * feats:].reshape(windows, count, heads, head_dim).astype(jnp.float32)
    scores = jnp.einsum('wthd,wshd->whts', query, keys, precision=lax.Precision.HIGHEST) * head_dim ** (-0.5)
    same = region[:, None] == region[None, :]
    scores = jnp.where(same[None, None], scores, -1e+30)
    top = lax.optimization_barrier(jnp.max(scores, axis=-1, keepdims=True))
    expo = jnp.exp(scores - top)
    weights = (expo / lax.optimization_barrier(jnp.sum(expo, axis=-1, keepdims=True))).astype(jnp.bfloat16)
    mixed = jnp.einsum('whts,wshd->wthd', weights.astype(jnp.float32), values, precision=lax.Precision.HIGHEST)
    return mixed.astype(jnp.bfloat16).reshape(windows, count, feats)

def window_branch(tiles_row, region, gain, qkv_weight, proj_weight, heads):
    windows, count, feats = tiles_row.shape
    flat = tiles_row.reshape(windows * count, feats)
    qkv = jnp.dot(flat, qkv_weight, preferred_element_type=jnp.float32).astype(jnp.bfloat16)
    mixed = attend(qkv.reshape(windows, count, 3 * feats), region, heads)
    projected = jnp.dot(mixed.reshape(windows * count, feats), proj_weight, preferred_element_type=jnp.float32)
    return layer_norm(projected, gain).astype(jnp.bfloat16).reshape(windows, count, feats)

def shifted_block(field, gain, qkv_weight, proj_weight, heads):
    levels, height, width, feats = field.shape
    lat_shift = WIN_LAT // 2
    lon_shift = WIN_LON // 2
    rolled = jnp.roll(field, (-lat_shift, -lon_shift), (1, 2))
    tiles = window_tiles(rolled, WIN_LAT, WIN_LON)
    count = WIN_LEV * WIN_LAT * WIN_LON
    lat_pos = jnp.arange(count, dtype=jnp.int32) // WIN_LON % WIN_LAT
    rows = jnp.arange(height // WIN_LAT, dtype=jnp.int32)[:, None] * WIN_LAT + lat_pos[None, :]
    region = (rows >= height - lat_shift).astype(jnp.int32)

    def one_row(pair):
        return window_branch(pair[0], pair[1], gain, qkv_weight, proj_weight, heads)
    branch = lax.map(one_row, (tiles, region))
    back = jnp.roll(tiles_field(branch, levels, WIN_LAT, WIN_LON), (lat_shift, lon_shift), (1, 2))
    return (field.astype(jnp.float32) + back.astype(jnp.float32)).astype(jnp.bfloat16)

def merge_patches(field, merge_weight):
    levels, height, width, feats = field.shape
    quads = field.reshape(levels, height // 2, 2, width // 2, 2, feats).transpose(0, 1, 3, 4, 2, 5)
    quads = quads.reshape(levels * (height // 2) * (width // 2), 4 * feats)
    merged = jnp.dot(quads, merge_weight, preferred_element_type=jnp.float32).astype(jnp.bfloat16)
    return merged.reshape(levels, height // 2, width // 2, merge_weight.shape[1])

def reference(latent_field, gain_one, qkv_one, proj_one, merge_weight, gain_two, qkv_two, proj_two, decode_up, decode_skip):
    first = shifted_block(latent_field, gain_one, qkv_one, proj_one, HEADS_ONE)
    coarse = merge_patches(first, merge_weight)
    second = shifted_block(coarse, gain_two, qkv_two, proj_two, HEADS_TWO)
    upper = jnp.repeat(jnp.repeat(second, 2, axis=1), 2, axis=2)
    levels, height, width, feats = first.shape
    total = jnp.dot(upper.reshape(-1, upper.shape[3]), decode_up, preferred_element_type=jnp.float32)
    total = total + jnp.dot(first.reshape(-1, feats), decode_skip, preferred_element_type=jnp.float32)
    return total.astype(jnp.bfloat16).reshape(levels, height, width, decode_skip.shape[1])
```

```python
import functools

import jax
import jax.numpy as jnp
import numpy as np
from jax import lax
from jax.experimental import pallas as pl
from jax.experimental.pallas import tpu as pltpu
from jax.sharding import PartitionSpec as P

MESH = pl.DeviceIdType.MESH
F32, BF16 = jnp.float32, jnp.bfloat16

QKV1, PROJ1, MERGE, QKV2, PROJ2, UP, SKIP, ROWS = 0, 48, 64, 192, 384, 448, 480, 496
GROUPS = ((0, 64, 16), (64, 128, 16), (192, 192, 48), (384, 112, 16))


def one_hot(rows, cols, pairs):
    m = np.zeros((rows, cols), np.float32)
    for r, c in pairs:
        m[r, c] = 1.0
    return m


def grid(levels, rows, cols):
    return [(v, r, c) for v in range(levels) for r in rows for c in cols]


def orders():
    R = range
    own = lambda v, r, c: v * 288 + r * 24 + c

    def frame(v, r, c):
        wi, r = divmod(r - 3, 6)
        wj, c = divmod(c - 6, 12)
        return (wi * 2 + wj) * 144 + v * 72 + r * 12 + c

    def packed(parts, index):
        pairs, base = [], 0
        for tokens, room in parts:
            pairs += [(base + n, index(*t)) for n, t in enumerate(tokens)]
            base += room
        return base, pairs

    lat_x, lon_x, dia_x = grid(2, R(0, 3), R(6, 24)), grid(2, R(3, 12), R(0, 6)), grid(2, R(0, 3), R(0, 6))
    n, pairs = packed(((lat_x, 112), (lon_x, 112), (dia_x, 48)), own)
    pack_x = one_hot(n, 576, pairs)
    where = {}
    for v, r, c in grid(2, R(12), R(24)):
        where[(v, r, c)] = own(v, r, c)
    for i, (v, r, c) in enumerate(lat_x):
        where[(v, r + 12, c)] = 576 + i
    for i, (v, r, c) in enumerate(lon_x):
        where[(v, r, c + 24)] = 688 + i
    for i, (v, r, c) in enumerate(dia_x):
        where[(v, r + 12, c + 24)] = 800 + i
    to_win = one_hot(576, 848, [(frame(*t), where[t]) for t in grid(2, R(3, 15), R(6, 30))])

    flat, flon, fdia = grid(2, R(3, 6), R(12, 30)), grid(2, R(6, 15), R(6, 12)), grid(2, R(3, 6), R(6, 12))
    blat, blon, bdia = grid(2, R(12, 15), R(6, 24)), grid(2, R(3, 12), R(24, 30)), grid(2, R(12, 15), R(24, 30))
    n, pairs = packed(((flat, 112), (flon, 112), (fdia, 48), (blat, 112), (blon, 112), (bdia, 48)), frame)
    pack_f = one_hot(n, 576, pairs)
    fwd, bwd = {}, {}
    for t in grid(2, R(3, 15), R(6, 30)):
        fwd[t], bwd[t] = 272 + frame(*t), frame(*t)
    for i, (v, r, c) in enumerate(flat):
        fwd[(v, r + 12, c)] = i
    for i, (v, r, c) in enumerate(flon):
        fwd[(v, r, c + 24)] = 112 + i
    for i, (v, r, c) in enumerate(fdia):
        fwd[(v, r + 12, c + 24)] = 224 + i
    for i, (v, r, c) in enumerate(blat):
        bwd[(v, r - 12, c)] = 576 + i
    for i, (v, r, c) in enumerate(blon):
        bwd[(v, r, c - 24)] = 688 + i
    for i, (v, r, c) in enumerate(bdia):
        bwd[(v, r - 12, c - 24)] = 800 + i
    quads = one_hot(576, 848, [
        ((dj * 2 + di) * 144 + v * 72 + r * 12 + c, fwd[(v, 6 + 2 * r + di, 12 + 2 * c + dj)])
        for di in R(2) for dj in R(2) for v, r, c in grid(2, R(6), R(12))
    ])
    to_own = one_hot(576, 848, [(own(*t), bwd[t]) for t in grid(2, R(12), R(24))])

    win = lambda v, r, c: v * 72 + r * 12 + c
    ulat, ulon, udia = grid(2, R(3, 6), R(0, 6)), grid(2, R(0, 3), R(6, 12)), grid(2, R(3, 6), R(6, 12))
    n, pairs = packed(((ulat, 48), (ulon, 48), (udia, 48)), win)
    pack_u = one_hot(n, 144, pairs)
    home = {}
    for v, r, c in grid(2, R(0, 3), R(0, 6)):
        home[(v, r + 3, c + 6)] = win(v, r, c)
    for i, (v, r, c) in enumerate(ulat):
        home[(v, r - 3, c + 6)] = 144 + i
    for i, (v, r, c) in enumerate(ulon):
        home[(v, r + 3, c - 6)] = 192 + i
    for i, (v, r, c) in enumerate(udia):
        home[(v, r - 3, c - 6)] = 240 + i
    up = one_hot(576, 288, [(own(v, r, c), home[(v, r // 2, c // 2)]) for v, r, c in grid(2, R(12), R(24))])
    return pack_x, to_win, pack_f, quads, to_own, pack_u, up


def dot(a, b):
    return jnp.dot(a, b, preferred_element_type=F32)


def norm(values, gain):
    center = values - jnp.mean(values, axis=-1, keepdims=True)
    spread = jnp.mean(center * center, axis=-1, keepdims=True)
    return center * lax.rsqrt(spread + 1e-05) * gain


class Net:
    def __init__(self, w, send, recv):
        self.w, self.send, self.recv = w, send, recv
        lat, lon = lax.axis_index("lat"), lax.axis_index("lon")
        y, xl = lat // 2, lat % 2
        xh, z, k = lon // 16, (lon // 2) % 8, lon % 2
        self.xh, self.z, self.k = xh, z, k
        self.color = (y + 2 * xl) % 4
        self.dev = {
            "cross": (y * 2 + 1 - xl, (1 - xh) * 16 + z * 2 + k),
            "pair": (y * 2 + 1 - xl, lon),
            "yp": (((y + 1) % 4) * 2 + xl, lon),
            "ym": (((y + 3) % 4) * 2 + xl, lon),
            "core": (lat, lon + 1 - 2 * k),
        }
        for s in range(1, 8):
            self.dev["z", s] = (lat, xh * 16 + ((z + s) % 8) * 2 + k)
        for a in (-1, 0, 1):
            for b in (-1, 0, 1):
                if a * b >= 0 and (a, b) != (0, 0):
                    self.dev["halo", a, b] = ((lat + a + 8) % 8, (lon + b + 32) % 32)
        self.used = 0
        self.open = []

    def to(self, name):
        lat, lon = self.dev[name]
        return {"lat": lat, "lon": lon}

    def sems(self):
        self.used += 1
        return self.used - 1

    def copy(self, src, dst, name, sem):
        d = pltpu.make_async_remote_copy(
            src_ref=src, dst_ref=dst, send_sem=self.send.at[self.sems()], recv_sem=self.recv.at[sem],
            device_id=self.to(name), device_id_type=MESH,
        )
        d.start()
        self.open.append(d)

    def wait(self, ref, sem):
        pltpu.make_async_remote_copy(
            src_ref=ref, dst_ref=ref, send_sem=self.send.at[0], recv_sem=self.recv.at[sem],
            device_id=self.to("core"), device_id_type=MESH,
        ).wait_recv()

    def finish(self):
        for d in self.open:
            d.wait_send()

    def step(self, c, t):
        w, xh, k, z = self.w, self.xh, self.k, self.z
        a, n, qu = GROUPS[c]
        com = n - 4 * qu
        quarter = lambda q: pl.ds(pl.multiple_of(a + q * qu, 16), qu)
        q, q2 = self.color, (self.color + 2) % 4
        common, full = pl.ds(a + 4 * qu, com), pl.ds(a, n)
        sem = lambda i: 16 * c + i
        if t == 0:
            for s in range(1, 8):
                mine = w.at[xh, z, k, quarter(q)]
                self.copy(mine, mine, ("z", s), sem(0))
                if com:
                    mine = w.at[xh, z, k, common]
                    self.copy(mine, mine, ("z", s), sem(1))
        elif t == 1:
            self.wait(w.at[xh, pl.ds(0, 7), k, quarter(q)], sem(0))
            mine = w.at[xh, :, k, quarter(q)]
            self.copy(mine, mine, "cross", sem(2))
            for name in ("pair", "yp", "ym"):
                self.copy(mine, mine, name, sem(3))
            if com:
                self.wait(w.at[xh, pl.ds(0, 7), k, common], sem(1))
                mine = w.at[xh, :, k, common]
                self.copy(mine, mine, "cross", sem(4))
        elif t == 2:
            mine = w.at[1 - xh, :, k, quarter(q2)]
            self.wait(mine, sem(2))
            for name in ("pair", "yp", "ym"):
                self.copy(mine, mine, name, sem(5))
        elif t == 3:
            self.wait(w.at[xh, :, k, pl.ds(a, 3 * qu)], sem(3))
            mine = w.at[xh, :, k, full]
            self.copy(mine, mine, "core", sem(6))
        elif t == 4:
            if com:
                self.wait(w.at[1 - xh, :, k, common], sem(4))
            self.wait(w.at[xh, :, k, pl.ds(a, 3 * qu)], sem(5))
            mine = w.at[1 - xh, :, k, full]
            self.copy(mine, mine, "core", sem(7))
        else:
            self.wait(w.at[xh, :, k, full], sem(6))
            self.wait(w.at[xh, :, k, full], sem(7))

    def halo(self, src, dst, base, at, to, sign, sem):
        for i, (a, b) in enumerate(((1, 0), (0, 1), (1, 1))):
            rows = at[i + 1] - at[i]
            self.copy(
                src.at[:, pl.ds(base + at[i], rows)], dst.at[:, pl.ds(to + at[i], rows)],
                ("halo", sign * a, sign * b), sem,
            )


PLAN = (
    (0, 0), (0, 1), (1, 0), (0, 2), (0, 3), (0, 4), (1, 1), (2, 0), (0, 5),
    (1, 2), (1, 3), (2, 1), (1, 4), (3, 0), (1, 5), (2, 2), (2, 3), (3, 1), (2, 4), (2, 5), (3, 2), (3, 3), (3, 4), (3, 5),
)


def kernel(
    x_in, gain1, gain2, qkv1, proj1, merge, qkv2, proj2, up_w, skip_w,
    pack_x, to_win, pack_f, quads, to_own, pack_u, up_m, out,
    w, xe, snd_x, xw, qkv, fe, snd_f, qd, coarse, big, mixed, ue, snd_u, skipped, bias, send, recv, local,
):
    net = Net(w, send, recv)
    lat = lax.axis_index("lat")

    loads = []

    def load(src, dst):
        d = pltpu.make_async_copy(src, dst, local.at[len(loads)])
        d.start()
        loads.append(d)

    row = 0
    for ref in (qkv1, proj1, merge, qkv2, proj2, up_w, skip_w):
        rows, cols = ref.shape
        for b in range(cols // 512):
            load(ref.at[:, pl.ds(512 * b, 512)], w.at[net.xh, net.z, net.k, pl.ds(row, rows)])
            row += rows
    load(x_in, xe.at[:, pl.ds(0, 576)])
    for d in loads:
        d.wait()
    barrier = pltpu.get_barrier_semaphore()
    for name in net.dev:
        pl.semaphore_signal(barrier, inc=1, device_id=net.to(name), device_id_type=MESH)
    pl.semaphore_wait(barrier, len(net.dev))

    plan = list(PLAN)

    def serve(count):
        for _ in range(min(count, len(plan))):
            net.step(*plan.pop(0))

    def need(c):
        while (c, 5) in plan:
            serve(1)

    serve(1)
    for g in range(2):
        snd_x[g] = dot(pack_x[...], xe[g, pl.ds(0, 576)]).astype(BF16)
    net.halo(snd_x, xe, 0, (0, 112, 224, 272), 576, -1, 100)
    serve(2)

    col = lax.broadcasted_iota(jnp.int32, (288, 144), 1)
    rowi = lax.broadcasted_iota(jnp.int32, (288, 144), 0)
    rowi = jnp.where(rowi >= 144, rowi - 144, rowi)
    low = lambda t: jnp.where(t >= 72, t - 72, t) >= 36
    apart = jnp.logical_xor(low(rowi), low(col))
    last = (lat == 7).astype(F32)
    bias[0] = jnp.zeros((288, 144), F32)
    bias[1] = jnp.where(apart, -1e30, 0.0) * last
    left = (lax.broadcasted_iota(jnp.int32, (144, 128), 1) < 64).astype(F32)
    left16 = left.astype(BF16)
    right16 = (1.0 - left).astype(BF16)
    ones = jnp.ones((144, 128), BF16)

    serve(2)
    net.wait(xe.at[:, pl.ds(576, 272)], 100)
    for g in range(2):
        xw[pl.ds(576 * g, 576)] = dot(to_win[...], xe[g]).astype(BF16)

    def weight(at, rows):
        return w[:, :, :, pl.ds(at, rows), :].reshape(32 * rows, 512)

    def attend(src, at, rows, cols, pairs, which, dst):
        for h in range(pairs):
            lanes = pl.ds(128 * h, 128)
            q = src[rows, pl.ds(at[0] + 128 * h, 128)]
            keys = src[rows, pl.ds(at[1] + 128 * h, 128)]
            vals = src[rows, pl.ds(at[2] + 128 * h, 128)]
            q = jnp.concatenate([q * left16, q * right16], axis=0)
            s = lax.dot_general(q, keys, (((1,), (1,)), ((), ())), preferred_element_type=F32) + bias[which]
            p = jnp.exp(s - jnp.max(s, axis=-1, keepdims=True)).astype(BF16)
            o = dot(p, jnp.concatenate([vals, ones], axis=1))
            o = o[:, :128] / o[:, 128:]
            dst[rows, lanes] = jnp.where(left > 0.5, o[:144], o[144:]).astype(BF16)

    need(0)
    for b in range(3):
        wb = weight(QKV1 + 16 * b, 16)

        def one(i, _):
            rows = pl.ds(pl.multiple_of(i * 288, 16), 288)
            o = dot(xw[rows], wb)
            qkv[rows, pl.ds(512 * b, 512)] = (o * 0.125 if b == 0 else o).astype(BF16)
            return 0

        lax.fori_loop(0, 4, one, 0)
        serve(1)

    for part in range(4):

        def window(i, _):
            n = part * 2 + i
            rows = pl.ds(pl.multiple_of(n * 144, 16), 144)
            attend(qkv, (0, 512, 1024), rows, 512, 4, part % 2, mixed)
            branch = norm(dot(mixed[rows, pl.ds(0, 512)], weight(PROJ1, 16)), gain1[...]).astype(BF16)
            inside = pl.ds(pl.multiple_of(272 + (n % 4) * 144, 16), 144)
            fe[part // 2, inside] = (xw[rows].astype(F32) + branch.astype(F32)).astype(BF16)
            return 0

        lax.fori_loop(0, 2, window, 0)
        serve(2)

    own = pl.ds(272, 576)
    for g in range(2):
        snd_f[g] = dot(pack_f[...], fe[g, own]).astype(BF16)
    net.halo(snd_f, fe, 0, (0, 112, 224, 272), 0, -1, 101)
    net.halo(snd_f, fe, 272, (0, 112, 224, 272), 848, 1, 102)
    serve(2)
    net.wait(fe.at[:, pl.ds(0, 272)], 101)
    for g in range(2):
        picked = dot(quads[...], fe[g, pl.ds(0, 848)]).astype(BF16)
        for q in range(4):
            qd[pl.ds(144 * g, 144), pl.ds(512 * q, 512)] = picked[144 * q : 144 * (q + 1)]
    need(1)
    for b in range(2):
        total = dot(qd[...], weight(MERGE + 64 * b, 64))
        coarse[:, pl.ds(512 * b, 512)] = total.astype(BF16)
        serve(1)

    net.wait(fe.at[:, pl.ds(848, 272)], 102)
    for g in range(2):
        xw[pl.ds(576 * g, 576)] = dot(to_own[...], fe[g, pl.ds(272, 848)]).astype(BF16)

    need(2)
    for b in range(6):
        o = dot(coarse[...], weight(QKV2 + 32 * b, 32))
        big[:, pl.ds(512 * b, 512)] = (o * 0.125 if b < 2 else o).astype(BF16)
    serve(1)

    def window2(g, _):
        rows = pl.ds(pl.multiple_of(g * 144, 16), 144)
        attend(big, (0, 1024, 2048), rows, 1024, 8, 1, mixed)
        return 0

    lax.fori_loop(0, 2, window2, 0)
    need(3)
    rows = pl.ds(0, 288)
    projected = jnp.concatenate([dot(mixed[rows], weight(PROJ2 + 32 * b, 32)) for b in range(2)], axis=1)
    branch = norm(projected, gain2[...]).astype(BF16)
    second = (coarse[...].astype(F32) + branch.astype(F32)).astype(BF16)
    term = dot(second, weight(UP, 32)).astype(BF16)
    for g in range(2):
        ue[g, pl.ds(0, 144)] = term[144 * g : 144 * (g + 1)]
        snd_u[g] = dot(pack_u[...], term[144 * g : 144 * (g + 1)]).astype(BF16)
    net.halo(snd_u, ue, 0, (0, 48, 96, 144), 144, 1, 103)

    def skip(i, _):
        rows = pl.ds(pl.multiple_of(i * 288, 16), 288)
        skipped[rows] = dot(xw[rows], weight(SKIP, 16))
        return 0

    lax.fori_loop(0, 4, skip, 0)
    net.wait(ue.at[:, pl.ds(144, 144)], 103)
    for g in range(2):
        out[g] = (skipped[pl.ds(576 * g, 576)] + dot(up_m[...], ue[g])).astype(BF16)
    net.finish()


def body(field, gain1, qkv1, proj1, merge, gain2, qkv2, proj2, up_w, skip_w):
    constants = [jnp.asarray(m, BF16) for m in orders()]
    hbm, vmem = pl.BlockSpec(memory_space=pl.ANY), pl.BlockSpec(memory_space=pltpu.VMEM)
    v = lambda *shape: pltpu.VMEM(shape, BF16)
    out = pl.pallas_call(
        kernel,
        out_shape=jax.ShapeDtypeStruct((2, 576, 512), BF16),
        in_specs=[hbm, vmem, vmem] + [hbm] * 7 + [vmem] * 7,
        out_specs=vmem,
        scratch_shapes=[
            v(2, 8, 2, ROWS, 512),
            v(2, 848, 512), v(2, 272, 512), v(1152, 512), v(1152, 1536),
            v(2, 1120, 512), v(2, 544, 512), v(288, 2048), v(288, 1024), v(288, 3072), v(1152, 1024),
            v(2, 288, 512), v(2, 144, 512),
            pltpu.VMEM((1152, 512), F32), pltpu.VMEM((2, 288, 144), F32),
            pltpu.SemaphoreType.DMA((128,)), pltpu.SemaphoreType.DMA((104,)), pltpu.SemaphoreType.DMA((24,)),
        ],
        compiler_params=pltpu.CompilerParams(collective_id=0, has_side_effects=True, vmem_limit_bytes=60 << 20),
    )(field.reshape(2, 576, 512), gain1.reshape(1, 512), gain2.reshape(1, 1024), qkv1, proj1, merge, qkv2, proj2, up_w, skip_w, *constants)
    return out.reshape(4, 12, 24, 512)


def solution(mesh):
    rows = P("lon", None)
    in_specs = (P(None, "lat", "lon", None), P(), rows, rows, rows, P(), rows, rows, rows, rows)
    return jax.shard_map(body, mesh=mesh, in_specs=in_specs, out_specs=P(None, "lat", "lon", None), check_vma=False)
```

```python
import functools

import jax
import jax.numpy as jnp
import numpy as np
from jax import lax
from jax.experimental import pallas as pl
from jax.experimental.pallas import tpu as pltpu
from jax.sharding import PartitionSpec as P

MESH = pl.DeviceIdType.MESH
F32, BF16 = jnp.float32, jnp.bfloat16

QKV1, PROJ1, MERGE, QKV2, PROJ2, UP, SKIP, ROWS = 0, 48, 64, 192, 384, 448, 480, 496
GROUPS = (
    (0, 64, "Q"),
    (64, 64, "Q"),
    (128, 128, "Q"),
    (256, 64, "H"),
    (320, 64, "H"),
    (384, 64, "X"),
    (448, 48, "C"),
)
ORDER = (
    0, ("packx",), 1, 2, 9, 18, ("win", 0), 3, 4, 10, 11, 27, 19, ("win", 1), 20, 5, 12, 28, 13, 6, 36, 29, 21, 7, 22,
    37, 45, 8, 14, ("qkv1_", 0, 0), 15, 38, 30, ("qkv1_", 0, 1), 31, ("qkv1_", 0, 2), ("att", 0, 0), 46, ("att", 0, 1),
    23, 24, ("att", 0, 2), 47, ("att", 0, 3), 16, 39, 40, 54, ("packf", 0), 17, 32, 33, 48, 49, ("qkv1_", 1, 0),
    ("qkv1_", 1, 1), 55, ("qkv1_", 1, 2), ("att", 1, 0), 41, 25, 50, 51, 56, ("att", 1, 1), 42, ("att", 1, 2), 26,
    ("att", 1, 3), 57, ("packf", 1), 34, ("quads", 0), ("merge", 0, 0), 58, 35, 43, ("merge", 0, 1), ("qkv2_", 0, 0),
    ("qkv2_", 0, 1), ("qkv2_", 0, 2), ("qkv2_", 0, 3), ("bwd", 0), ("bwd", 1), 44, ("qkv2_", 0, 4), ("qkv2_", 0, 5),
    ("att2_", 0, 0), 52, ("att2_", 0, 1), ("att2_", 0, 2), 59, 60, 61, ("att2_", 0, 3), 53, ("proj2_", 0), 62,
    ("up", 0), ("quads", 1), ("merge", 1, 0), ("merge", 1, 1), ("qkv2_", 1, 0), ("qkv2_", 1, 1), ("qkv2_", 1, 2),
    ("qkv2_", 1, 3), ("qkv2_", 1, 4), ("qkv2_", 1, 5), ("att2_", 1, 0), ("att2_", 1, 1), ("att2_", 1, 2),
    ("att2_", 1, 3), ("proj2_", 1), ("up", 1), ("own", 0), ("own", 1), ("skip", 0), ("fin", 0), ("skip", 1), ("fin", 1),
)


def one_hot(rows, cols, pairs):
    m = np.zeros((rows, cols), np.float32)
    for r, c in pairs:
        m[r, c] = 1.0
    return m


def grid(levels, rows, cols):
    return [(v, r, c) for v in range(levels) for r in rows for c in cols]


def orders():
    R = range
    own = lambda v, r, c: v * 288 + r * 24 + c

    def frame(v, r, c):
        wi, r = divmod(r - 3, 6)
        wj, c = divmod(c - 6, 12)
        return (wi * 2 + wj) * 144 + v * 72 + r * 12 + c

    def packed(parts, index):
        pairs, base = [], 0
        for tokens, room in parts:
            pairs += [(base + n, index(*t)) for n, t in enumerate(tokens)]
            base += room
        return base, pairs

    lat_x, lon_x, dia_x = grid(2, R(0, 3), R(6, 24)), grid(2, R(3, 12), R(0, 6)), grid(2, R(0, 3), R(0, 6))
    n, pairs = packed(((lat_x, 112), (lon_x, 112), (dia_x, 48)), own)
    pack_x = one_hot(n, 576, pairs)
    where = {}
    for v, r, c in grid(2, R(12), R(24)):
        where[(v, r, c)] = own(v, r, c)
    for i, (v, r, c) in enumerate(lat_x):
        where[(v, r + 12, c)] = 576 + i
    for i, (v, r, c) in enumerate(lon_x):
        where[(v, r, c + 24)] = 688 + i
    for i, (v, r, c) in enumerate(dia_x):
        where[(v, r + 12, c + 24)] = 800 + i
    to_win = one_hot(576, 848, [(frame(*t), where[t]) for t in grid(2, R(3, 15), R(6, 30))])

    flat, flon, fdia = grid(2, R(3, 6), R(12, 30)), grid(2, R(6, 15), R(6, 12)), grid(2, R(3, 6), R(6, 12))
    blat, blon, bdia = grid(2, R(12, 15), R(6, 24)), grid(2, R(3, 12), R(24, 30)), grid(2, R(12, 15), R(24, 30))
    n, pairs = packed(((flat, 112), (flon, 112), (fdia, 48), (blat, 112), (blon, 112), (bdia, 48)), frame)
    pack_f = one_hot(n, 576, pairs)
    fwd, bwd = {}, {}
    for t in grid(2, R(3, 15), R(6, 30)):
        fwd[t], bwd[t] = 272 + frame(*t), frame(*t)
    for i, (v, r, c) in enumerate(flat):
        fwd[(v, r + 12, c)] = i
    for i, (v, r, c) in enumerate(flon):
        fwd[(v, r, c + 24)] = 112 + i
    for i, (v, r, c) in enumerate(fdia):
        fwd[(v, r + 12, c + 24)] = 224 + i
    for i, (v, r, c) in enumerate(blat):
        bwd[(v, r - 12, c)] = 576 + i
    for i, (v, r, c) in enumerate(blon):
        bwd[(v, r, c - 24)] = 688 + i
    for i, (v, r, c) in enumerate(bdia):
        bwd[(v, r - 12, c - 24)] = 800 + i
    quads = one_hot(576, 848, [
        ((dj * 2 + di) * 144 + v * 72 + r * 12 + c, fwd[(v, 6 + 2 * r + di, 12 + 2 * c + dj)])
        for di in R(2) for dj in R(2) for v, r, c in grid(2, R(6), R(12))
    ])
    to_own = one_hot(576, 848, [(own(*t), bwd[t]) for t in grid(2, R(12), R(24))])

    win = lambda v, r, c: v * 72 + r * 12 + c
    ulat, ulon, udia = grid(2, R(3, 6), R(0, 6)), grid(2, R(0, 3), R(6, 12)), grid(2, R(3, 6), R(6, 12))
    n, pairs = packed(((ulat, 48), (ulon, 48), (udia, 48)), win)
    pack_u = one_hot(n, 144, pairs)
    home = {}
    for v, r, c in grid(2, R(0, 3), R(0, 6)):
        home[(v, r + 3, c + 6)] = win(v, r, c)
    for i, (v, r, c) in enumerate(ulat):
        home[(v, r - 3, c + 6)] = 144 + i
    for i, (v, r, c) in enumerate(ulon):
        home[(v, r + 3, c - 6)] = 192 + i
    for i, (v, r, c) in enumerate(udia):
        home[(v, r - 3, c - 6)] = 240 + i
    up = one_hot(576, 288, [(own(v, r, c), home[(v, r // 2, c // 2)]) for v, r, c in grid(2, R(12), R(24))])
    return pack_x, to_win, pack_f, quads, to_own, pack_u, up


def dot(a, b):
    return jnp.dot(a, b, preferred_element_type=F32)


def norm(values, gain):
    center = values - jnp.mean(values, axis=-1, keepdims=True)
    spread = jnp.mean(center * center, axis=-1, keepdims=True)
    return center * lax.rsqrt(spread + 1e-05) * gain


class Net:
    def __init__(self, w, send, recv):
        self.w, self.send, self.recv = w, send, recv
        lat, lon = lax.axis_index("lat"), lax.axis_index("lon")
        y, xl = lat // 2, lat % 2
        xh, z, k = lon // 16, (lon // 2) % 8, lon % 2
        self.xh, self.z, self.k = xh, z, k
        self.color, self.side = (y + 2 * xl) % 4, (y + xl) % 2
        self.dev = {
            "cross": (y * 2 + 1 - xl, (1 - xh) * 16 + z * 2 + k),
            "pair": (y * 2 + 1 - xl, lon),
            "yp": (((y + 1) % 4) * 2 + xl, lon),
            "ym": (((y + 3) % 4) * 2 + xl, lon),
            "core": (lat, lon + 1 - 2 * k),
        }
        for s in range(1, 8):
            self.dev["z", s] = (lat, xh * 16 + ((z + s) % 8) * 2 + k)
        for a in (-1, 0, 1):
            for b in (-1, 0, 1):
                if a * b >= 0 and (a, b) != (0, 0):
                    self.dev["halo", a, b] = ((lat + a + 8) % 8, (lon + b + 32) % 32)
        self.used = 0
        self.open = []

    def to(self, name):
        lat, lon = self.dev[name]
        return {"lat": lat, "lon": lon}

    def sems(self):
        self.used += 1
        return self.used - 1

    def copy(self, src, dst, name, sem):
        d = pltpu.make_async_remote_copy(
            src_ref=src, dst_ref=dst, send_sem=self.send.at[self.sems()], recv_sem=self.recv.at[sem],
            device_id=self.to(name), device_id_type=MESH,
        )
        d.start()
        self.open.append(d)

    def wait(self, ref, sem):
        pltpu.make_async_remote_copy(
            src_ref=ref, dst_ref=ref, send_sem=self.send.at[0], recv_sem=self.recv.at[sem],
            device_id=self.to("core"), device_id_type=MESH,
        ).wait_recv()

    def finish(self):
        for d in self.open:
            d.wait_send()

    def step(self, c, t):
        w, xh, k, z = self.w, self.xh, self.k, self.z
        a, n, kind = GROUPS[c]
        full = pl.ds(a, n)
        quarter = lambda q: pl.ds(pl.multiple_of(a + q % 4 * (n // 4), 16), n // 4)
        half = lambda q: pl.ds(pl.multiple_of(a + q % 2 * (n // 2), 16), n // 2)
        q = self.color
        fetch = {"Q": quarter(q), "H": half(self.side), "X": full, "C": full}[kind]
        over = {"Q": quarter(q), "H": half(self.side), "X": quarter(q), "C": full}[kind]
        theirs = {"Q": quarter(q + 2), "H": half(self.side + 1), "X": quarter(q + 2), "C": full}[kind]
        odd, even = (z + 1) % 2, z % 2
        halved = kind == "Q" and c == 0
        sem = lambda i: 14 * c + i

        def shard(s):
            at = (z + s) % 8
            return w.at[xh, at // 2, at % 2, k, fetch]

        def push(ref, name, i):
            self.copy(ref, ref, name, sem(i))

        def spread(x, rows, i, only=slice(None)):
            if kind == "H":
                at = rows.start
                push(w.at[x, pl.ds(0, 1), :, k, rows], "pair", i)
                push(w.at[x, pl.ds(1, 3), :, k, pl.ds(pl.multiple_of(at, 16), n // 4)], "yp", i)
                push(w.at[x, pl.ds(1, 3), :, k, pl.ds(pl.multiple_of(at + n // 4, 16), n // 4)], "ym", i)
            else:
                for name in ("pair", "yp", "ym"):
                    push(w.at[x, :, only, k, rows], name, i)

        brought = pl.ds(a, n // 2 if kind == "H" else 3 * n // 4)
        if t == 0:
            for i, s in enumerate((1, 7, 3, 5)):
                push(shard(0), ("z", s), i)
        elif t == 1:
            self.wait(shard(7), sem(0))
            push(shard(7), ("z", 1), 4)
            self.wait(shard(1), sem(1))
            push(shard(1), ("z", 7), 5)
        elif t == 2:
            self.wait(shard(5), sem(2))
            self.wait(shard(3), sem(3))
            push(w.at[xh, :, odd, k, over], "cross", 7)
            if c % 2 == 0:
                push(shard(5), ("z", 1), 6)
            else:
                push(shard(3), ("z", 7), 6)
        elif t == 3:
            self.wait(shard(6), sem(4))
            self.wait(shard(2), sem(5))
            self.wait(shard(4), sem(6))
            push(w.at[xh, :, even, k, over], "cross", 8)
            if kind in "QH":
                spread(xh, fetch, 9)
            else:
                push(w.at[xh, :, :, k, full], "core", 12)
        elif t == 4:
            self.wait(w.at[1 - xh, :, odd, k, theirs], sem(7))
            if halved:
                spread(1 - xh, theirs, 10, odd)
        elif t == 5:
            self.wait(w.at[1 - xh, :, even, k, theirs], sem(8))
            if kind == "C":
                push(w.at[1 - xh, :, :, k, full], "core", 13)
            else:
                spread(1 - xh, theirs, 11, even if halved else slice(None))
        elif t == 6:
            if kind in "QH":
                self.wait(w.at[xh, :, :, k, brought], sem(9))
                push(w.at[xh, :, :, k, full], "core", 12)
        elif t == 7:
            if halved:
                self.wait(w.at[xh, :, 0, k, brought], sem(10))
                self.wait(w.at[xh, :, 0, k, brought], sem(11))
            elif kind != "C":
                self.wait(w.at[xh, :, :, k, brought], sem(11))
            if kind != "C":
                push(w.at[1 - xh, :, :, k, full], "core", 13)
        else:
            self.wait(w.at[xh, :, :, k, full], sem(12))
            self.wait(w.at[xh, :, :, k, full], sem(13))

    def halo(self, src, dst, base, at, to, sign, sem):
        for i, (a, b) in enumerate(((1, 0), (0, 1), (1, 1))):
            rows = at[i + 1] - at[i]
            self.copy(
                src.at[pl.ds(base + at[i], rows)], dst.at[pl.ds(to + at[i], rows)],
                ("halo", sign * a, sign * b), sem,
            )


def kernel(
    x_in, gain1, gain2, qkv1, proj1, merge, qkv2, proj2, up_w, skip_w,
    m0, m1, m2, m3, m4, m5, m6, out,
    pack_x, to_win, pack_f, to_quad, to_own, pack_u, up_m,
    w, xe, snd_x, xw, qkv, fe, snd_f, qd, coarse, big, mixed, ue, snd_u, skipped, bias, send, recv, local,
):
    net = Net(w, send, recv)
    lat = lax.axis_index("lat")

    loads = []

    def load(src, dst):
        d = pltpu.make_async_copy(src, dst, local.at[len(loads)])
        d.start()
        loads.append(d)
        return d

    row = 0
    for ref in (qkv1, proj1, merge, qkv2, proj2, up_w, skip_w):
        rows, cols = ref.shape
        for b in range(cols // 512):
            load(ref.at[:, pl.ds(512 * b, 512)], w.at[net.xh, net.z // 2, net.z % 2, net.k, pl.ds(row, rows)])
            row += rows
    shards = list(loads)
    field = load(x_in, xe.at[:, pl.ds(0, 576)])
    order = [load(a, b) for a, b in zip((m0, m1, m2, m3, m4, m5, m6), (pack_x, to_win, pack_f, to_quad, to_own, pack_u, up_m))]
    for d in shards:
        d.wait()
    barrier = pltpu.get_barrier_semaphore()
    for name in net.dev:
        pl.semaphore_signal(barrier, inc=1, device_id=net.to(name), device_id_type=MESH)
    field.wait()
    order[0].wait()
    for g in range(2):
        snd_x[g] = dot(pack_x[...], xe[g, pl.ds(0, 576)]).astype(BF16)
    pl.semaphore_wait(barrier, len(net.dev))


    col = lax.broadcasted_iota(jnp.int32, (288, 144), 1)
    rowi = lax.broadcasted_iota(jnp.int32, (288, 144), 0)
    rowi = jnp.where(rowi >= 144, rowi - 144, rowi)
    low = lambda t: jnp.where(t >= 72, t - 72, t) >= 36
    apart = jnp.logical_xor(low(rowi), low(col))
    last = (lat == 7).astype(F32)
    bias[...] = jnp.where(apart, -1e30, 0.0) * last
    left = (lax.broadcasted_iota(jnp.int32, (144, 128), 1) < 64).astype(F32)
    left16 = left.astype(BF16)
    right16 = (1.0 - left).astype(BF16)
    ones = jnp.ones((144, 128), BF16)
    late = []

    def ready(i):
        if i not in late:
            late.append(i)
            order[i].wait()

    def weight(at, rows):
        return w[:, :, :, :, pl.ds(at, rows), :].reshape(32 * rows, 512)

    def attend(src, at, rows, heads, masked, dst):
        scores = []
        for h in heads:
            q = src[rows, pl.ds(at[0] + 128 * h, 128)]
            keys = src[rows, pl.ds(at[1] + 128 * h, 128)]
            q = jnp.concatenate([q * left16, q * right16], axis=0)
            s = lax.dot_general(q, keys, (((1,), (1,)), ((), ())), preferred_element_type=F32)
            scores.append(s + bias[...] if masked else s)
        parts = [jnp.exp(s - jnp.max(s, axis=-1, keepdims=True)).astype(BF16) for s in scores]
        for h, p in zip(heads, parts):
            vals = src[rows, pl.ds(at[2] + 128 * h, 128)]
            o = dot(p, jnp.concatenate([vals, ones], axis=1))
            o = o[:, :128] / o[:, 128:]
            dst[rows, pl.ds(128 * h, 128)] = jnp.where(left > 0.5, o[:144], o[144:]).astype(BF16)

    field_at, first_at, term_at = (0, 112, 224, 272), (0, 112, 224, 272), (0, 48, 96, 144)

    def packx():
        for g in range(2):
            net.halo(snd_x.at[g], xe.at[g], 0, field_at, 576, -1, 140 + g)

    def win(g):
        ready(1)
        net.wait(xe.at[g, pl.ds(576, 272)], 140 + g)
        xw[g] = dot(to_win[...], xe[g]).astype(BF16)

    def qkv1_(g, b):
        def one(i, _):
            rows = pl.ds(pl.multiple_of(i * 288, 16), 288)
            o = dot(xw[g, rows], weight(QKV1 + 16 * b, 16))
            qkv[rows, pl.ds(512 * b, 512)] = (o * 0.125 if b == 0 else o).astype(BF16)
            return 0

        lax.fori_loop(0, 2, one, 0)

    def att(g, n):
        rows, inside = pl.ds(n * 144, 144), pl.ds(272 + n * 144, 144)
        attend(qkv, (0, 512, 1024), rows, (0, 1), n >= 2, mixed)
        attend(qkv, (0, 512, 1024), rows, (2, 3), n >= 2, mixed)
        branch = norm(dot(mixed[rows, pl.ds(0, 512)], weight(PROJ1, 16)), gain1[...]).astype(BF16)
        fe[g, inside] = (xw[g, rows].astype(F32) + branch.astype(F32)).astype(BF16)

    def packf(g):
        ready(2)
        snd_f[g] = dot(pack_f[...], fe[g, pl.ds(272, 576)]).astype(BF16)
        net.halo(snd_f.at[g], fe.at[g], 0, first_at, 0, -1, 142 + g)

    def bwd(g):
        net.halo(snd_f.at[g], fe.at[g], 272, first_at, 848, 1, 144 + g)

    def quads(g):
        ready(3)
        net.wait(fe.at[g, pl.ds(0, 272)], 142 + g)
        picked = dot(to_quad[...], fe[g, pl.ds(0, 848)]).astype(BF16)
        for q in range(4):
            qd[:, pl.ds(512 * q, 512)] = picked[144 * q : 144 * (q + 1)]

    def merge_(g, b):
        coarse[g, :, pl.ds(512 * b, 512)] = dot(qd[...], weight(MERGE + 64 * b, 64)).astype(BF16)

    def qkv2_(g, b):
        o = dot(coarse[g], weight(QKV2 + 32 * b, 32))
        big[:, pl.ds(512 * b, 512)] = (o * 0.125 if b < 2 else o).astype(BF16)

    def att2_(g, i):
        attend(big, (0, 1024, 2048), pl.ds(0, 144), (2 * i, 2 * i + 1), True, mixed)

    def proj2_(g):
        projected = jnp.concatenate([dot(mixed[pl.ds(0, 144)], weight(PROJ2 + 32 * b, 32)) for b in range(2)], axis=1)
        branch = norm(projected, gain2[...]).astype(BF16)
        coarse[g] = (coarse[g].astype(F32) + branch.astype(F32)).astype(BF16)

    def up(g):
        ready(5)
        term = dot(coarse[g], weight(UP, 32)).astype(BF16)
        ue[g, pl.ds(0, 144)] = term
        snd_u[g] = dot(pack_u[...], term).astype(BF16)
        net.halo(snd_u.at[g], ue.at[g], 0, term_at, 144, 1, 146 + g)

    def own(g):
        ready(4)
        net.wait(fe.at[g, pl.ds(848, 272)], 144 + g)
        xw[g] = dot(to_own[...], fe[g, pl.ds(272, 848)]).astype(BF16)

    def skip(g):
        def one(i, _):
            rows = pl.ds(pl.multiple_of(i * 288, 16), 288)
            skipped[g, rows] = dot(xw[g, rows], weight(SKIP, 16))
            return 0

        lax.fori_loop(0, 2, one, 0)

    def fin(g):
        ready(6)
        net.wait(ue.at[g, pl.ds(144, 144)], 146 + g)
        out[g] = (skipped[g] + dot(up_m[...], ue[g])).astype(BF16)

    work = dict(
        packx=packx, win=win, qkv1_=qkv1_, att=att, packf=packf, bwd=bwd, quads=quads, merge=merge_,
        qkv2_=qkv2_, att2_=att2_, proj2_=proj2_, up=up, own=own, skip=skip, fin=fin,
    )
    for item in ORDER:
        if isinstance(item, int):
            net.step(item // 9, item % 9)
        else:
            work[item[0]](*item[1:])
    net.finish()


def body(field, gain1, qkv1, proj1, merge, gain2, qkv2, proj2, up_w, skip_w):
    constants = [jnp.asarray(m, BF16) for m in orders()]
    hbm, vmem = pl.BlockSpec(memory_space=pl.ANY), pl.BlockSpec(memory_space=pltpu.VMEM)
    v = lambda *shape: pltpu.VMEM(shape, BF16)
    out = pl.pallas_call(
        kernel,
        out_shape=jax.ShapeDtypeStruct((2, 576, 512), BF16),
        in_specs=[hbm, vmem, vmem] + [hbm] * 14,
        out_specs=vmem,
        scratch_shapes=[v(*m.shape) for m in constants] + [
            v(2, 4, 2, 2, ROWS, 512),
            v(2, 848, 512), v(2, 272, 512), v(2, 576, 512), v(576, 1536),
            v(2, 1120, 512), v(2, 544, 512), v(144, 2048), v(2, 144, 1024), v(144, 3072), v(576, 1024),
            v(2, 288, 512), v(2, 144, 512),
            pltpu.VMEM((2, 576, 512), F32), pltpu.VMEM((288, 144), F32),
            pltpu.SemaphoreType.DMA((200,)), pltpu.SemaphoreType.DMA((148,)), pltpu.SemaphoreType.DMA((24,)),
        ],
        compiler_params=pltpu.CompilerParams(collective_id=0, has_side_effects=True, vmem_limit_bytes=60 << 20),
    )(field.reshape(2, 576, 512), gain1.reshape(1, 512), gain2.reshape(1, 1024), qkv1, proj1, merge, qkv2, proj2, up_w, skip_w, *constants)
    return out.reshape(4, 12, 24, 512)


def solution(mesh):
    rows = P("lon", None)
    in_specs = (P(None, "lat", "lon", None), P(), rows, rows, rows, P(), rows, rows, rows, rows)
    return jax.shard_map(body, mesh=mesh, in_specs=in_specs, out_specs=P(None, "lat", "lon", None), check_vma=False)
```

```python
import functools

import jax
import jax.numpy as jnp
import numpy as np
from jax import lax
from jax.experimental import pallas as pl
from jax.experimental.pallas import tpu as pltpu
from jax.sharding import PartitionSpec as P

MESH = pl.DeviceIdType.MESH
F32, BF16 = jnp.float32, jnp.bfloat16

QKV1, PROJ1, MERGE, QKV2, PROJ2, UP, SKIP, ROWS = 0, 48, 64, 192, 384, 448, 480, 496
GROUPS = (
    (0, 64, "Q"),
    (64, 64, "Q"),
    (128, 128, "Q"),
    (256, 64, "H"),
    (320, 64, "H"),
    (384, 64, "X"),
    (448, 48, "C"),
)
ORDER = (
    0, ("packx",), 1, 2, 9, 18, ("win", 0), 3, 4, 10, 11, 27, 19, ("win", 1), 20, 5, 12, 28, 13, 6, 36, 29, 21, 7, 22,
    37, 45, 8, 14, ("qkv1_", 0, 0), 15, 38, 30, ("qkv1_", 0, 1), 31, ("qkv1_", 0, 2), ("att", 0, 0), 46, ("att", 0, 1),
    23, 24, ("att", 0, 2), 47, ("att", 0, 3), 16, 39, 40, 54, ("packf", 0), 17, 32, 33, 48, 49, ("qkv1_", 1, 0),
    ("qkv1_", 1, 1), 55, ("qkv1_", 1, 2), ("att", 1, 0), 41, 25, 50, 51, 56, ("att", 1, 1), 42, ("att", 1, 2), 26,
    ("att", 1, 3), 57, ("packf", 1), 34, ("quads", 0), ("merge", 0, 0), 58, 35, 43, ("merge", 0, 1), ("qkv2_", 0, 0),
    ("qkv2_", 0, 1), ("qkv2_", 0, 2), ("qkv2_", 0, 3), ("bwd", 0), ("bwd", 1), 44, ("qkv2_", 0, 4), ("qkv2_", 0, 5),
    ("att2_", 0, 0), 52, ("att2_", 0, 1), ("att2_", 0, 2), 59, 60, 61, ("att2_", 0, 3), 53, ("proj2_", 0), 62,
    ("up", 0), ("quads", 1), ("merge", 1, 0), ("merge", 1, 1), ("qkv2_", 1, 0), ("qkv2_", 1, 1), ("qkv2_", 1, 2),
    ("qkv2_", 1, 3), ("qkv2_", 1, 4), ("qkv2_", 1, 5), ("att2_", 1, 0), ("att2_", 1, 1), ("att2_", 1, 2),
    ("att2_", 1, 3), ("proj2_", 1), ("up", 1), ("own", 0), ("own", 1), ("skip", 0), ("fin", 0), ("skip", 1), ("fin", 1),
)


def one_hot(rows, cols, pairs):
    m = np.zeros((rows, cols), np.float32)
    for r, c in pairs:
        m[r, c] = 1.0
    return m


def grid(levels, rows, cols):
    return [(v, r, c) for v in range(levels) for r in rows for c in cols]


def orders():
    R = range
    own = lambda v, r, c: v * 288 + r * 24 + c

    def frame(v, r, c):
        wi, r = divmod(r - 3, 6)
        wj, c = divmod(c - 6, 12)
        return (wi * 2 + wj) * 144 + v * 72 + r * 12 + c

    def packed(parts, index):
        pairs, base = [], 0
        for tokens, room in parts:
            pairs += [(base + n, index(*t)) for n, t in enumerate(tokens)]
            base += room
        return base, pairs

    lat_x, lon_x, dia_x = grid(2, R(0, 3), R(6, 24)), grid(2, R(3, 12), R(0, 6)), grid(2, R(0, 3), R(0, 6))
    n, pairs = packed(((lat_x, 112), (lon_x, 112), (dia_x, 48)), own)
    pack_x = one_hot(n, 576, pairs)
    where = {}
    for v, r, c in grid(2, R(12), R(24)):
        where[(v, r, c)] = own(v, r, c)
    for i, (v, r, c) in enumerate(lat_x):
        where[(v, r + 12, c)] = 576 + i
    for i, (v, r, c) in enumerate(lon_x):
        where[(v, r, c + 24)] = 688 + i
    for i, (v, r, c) in enumerate(dia_x):
        where[(v, r + 12, c + 24)] = 800 + i
    to_win = one_hot(576, 848, [(frame(*t), where[t]) for t in grid(2, R(3, 15), R(6, 30))])

    flat, flon, fdia = grid(2, R(3, 6), R(12, 30)), grid(2, R(6, 15), R(6, 12)), grid(2, R(3, 6), R(6, 12))
    blat, blon, bdia = grid(2, R(12, 15), R(6, 24)), grid(2, R(3, 12), R(24, 30)), grid(2, R(12, 15), R(24, 30))
    n, pairs = packed(((flat, 112), (flon, 112), (fdia, 48), (blat, 112), (blon, 112), (bdia, 48)), frame)
    pack_f = one_hot(n, 576, pairs)
    fwd, bwd = {}, {}
    for t in grid(2, R(3, 15), R(6, 30)):
        fwd[t], bwd[t] = 272 + frame(*t), frame(*t)
    for i, (v, r, c) in enumerate(flat):
        fwd[(v, r + 12, c)] = i
    for i, (v, r, c) in enumerate(flon):
        fwd[(v, r, c + 24)] = 112 + i
    for i, (v, r, c) in enumerate(fdia):
        fwd[(v, r + 12, c + 24)] = 224 + i
    for i, (v, r, c) in enumerate(blat):
        bwd[(v, r - 12, c)] = 576 + i
    for i, (v, r, c) in enumerate(blon):
        bwd[(v, r, c - 24)] = 688 + i
    for i, (v, r, c) in enumerate(bdia):
        bwd[(v, r - 12, c - 24)] = 800 + i
    quads = one_hot(576, 848, [
        ((dj * 2 + di) * 144 + v * 72 + r * 12 + c, fwd[(v, 6 + 2 * r + di, 12 + 2 * c + dj)])
        for di in R(2) for dj in R(2) for v, r, c in grid(2, R(6), R(12))
    ])
    to_own = one_hot(576, 848, [(own(*t), bwd[t]) for t in grid(2, R(12), R(24))])

    win = lambda v, r, c: v * 72 + r * 12 + c
    ulat, ulon, udia = grid(2, R(3, 6), R(0, 6)), grid(2, R(0, 3), R(6, 12)), grid(2, R(3, 6), R(6, 12))
    n, pairs = packed(((ulat, 48), (ulon, 48), (udia, 48)), win)
    pack_u = one_hot(n, 144, pairs)
    home = {}
    for v, r, c in grid(2, R(0, 3), R(0, 6)):
        home[(v, r + 3, c + 6)] = win(v, r, c)
    for i, (v, r, c) in enumerate(ulat):
        home[(v, r - 3, c + 6)] = 144 + i
    for i, (v, r, c) in enumerate(ulon):
        home[(v, r + 3, c - 6)] = 192 + i
    for i, (v, r, c) in enumerate(udia):
        home[(v, r - 3, c - 6)] = 240 + i
    up = one_hot(576, 288, [(own(v, r, c), home[(v, r // 2, c // 2)]) for v, r, c in grid(2, R(12), R(24))])
    return pack_x, to_win, pack_f, quads, to_own, pack_u, up


def dot(a, b):
    return jnp.dot(a, b, preferred_element_type=F32)


def norm(values, gain):
    center = values - jnp.mean(values, axis=-1, keepdims=True)
    spread = jnp.mean(center * center, axis=-1, keepdims=True)
    return center * lax.rsqrt(spread + 1e-05) * gain


class Net:
    def __init__(self, w, send, recv):
        self.w, self.send, self.recv = w, send, recv
        lat, lon = lax.axis_index("lat"), lax.axis_index("lon")
        y, xl = lat // 2, lat % 2
        xh, z, k = lon // 16, (lon // 2) % 8, lon % 2
        self.xh, self.z, self.k = xh, z, k
        self.color, self.side = (y + 2 * xl) % 4, (y + xl) % 2
        self.dev = {
            "cross": (y * 2 + 1 - xl, (1 - xh) * 16 + z * 2 + k),
            "pair": (y * 2 + 1 - xl, lon),
            "yp": (((y + 1) % 4) * 2 + xl, lon),
            "ym": (((y + 3) % 4) * 2 + xl, lon),
            "core": (lat, lon + 1 - 2 * k),
        }
        for s in (1, 3, 5, 7):
            self.dev["z", s] = (lat, xh * 16 + ((z + s) % 8) * 2 + k)
        for a in (-1, 0, 1):
            for b in (-1, 0, 1):
                if a * b >= 0 and (a, b) != (0, 0):
                    self.dev["halo", a, b] = ((lat + a + 8) % 8, (lon + b + 32) % 32)
        self.used = 0
        self.open = []

    def to(self, name):
        lat, lon = self.dev[name]
        return {"lat": lat, "lon": lon}

    def sems(self):
        self.used += 1
        return self.used - 1

    def copy(self, src, dst, name, sem):
        d = pltpu.make_async_remote_copy(
            src_ref=src, dst_ref=dst, send_sem=self.send.at[self.sems()], recv_sem=self.recv.at[sem],
            device_id=self.to(name), device_id_type=MESH,
        )
        d.start()
        self.open.append(d)

    def wait(self, ref, sem):
        pltpu.make_async_remote_copy(
            src_ref=ref, dst_ref=ref, send_sem=self.send.at[0], recv_sem=self.recv.at[sem],
            device_id=self.to("core"), device_id_type=MESH,
        ).wait_recv()

    def finish(self):
        for d in self.open:
            d.wait_send()

    def step(self, c, t):
        w, xh, k, z = self.w, self.xh, self.k, self.z
        a, n, kind = GROUPS[c]
        full = pl.ds(a, n)
        quarter = lambda q: pl.ds(pl.multiple_of(a + q % 4 * (n // 4), 16), n // 4)
        half = lambda q: pl.ds(pl.multiple_of(a + q % 2 * (n // 2), 16), n // 2)
        q = self.color
        fetch = {"Q": quarter(q), "H": half(self.side), "X": full, "C": full}[kind]
        over = {"Q": quarter(q), "H": half(self.side), "X": quarter(q), "C": full}[kind]
        theirs = {"Q": quarter(q + 2), "H": half(self.side + 1), "X": quarter(q + 2), "C": full}[kind]
        odd, even = (z + 1) % 2, z % 2
        halved = kind == "Q" and c == 0
        sem = lambda i: 14 * c + i

        def shard(s):
            at = (z + s) % 8
            return w.at[xh, at // 2, at % 2, k, fetch]

        def push(ref, name, i):
            self.copy(ref, ref, name, sem(i))

        def spread(x, rows, i, only=slice(None)):
            if kind == "H":
                at = rows.start
                push(w.at[x, pl.ds(0, 1), :, k, rows], "pair", i)
                push(w.at[x, pl.ds(1, 3), :, k, pl.ds(pl.multiple_of(at, 16), n // 4)], "yp", i)
                push(w.at[x, pl.ds(1, 3), :, k, pl.ds(pl.multiple_of(at + n // 4, 16), n // 4)], "ym", i)
            else:
                for name in ("pair", "yp", "ym"):
                    push(w.at[x, :, only, k, rows], name, i)

        brought = pl.ds(a, n // 2 if kind == "H" else 3 * n // 4)
        if t == 0:
            for i, s in enumerate((1, 7, 3, 5)):
                push(shard(0), ("z", s), i)
        elif t == 1:
            self.wait(shard(7), sem(0))
            push(shard(7), ("z", 1), 4)
            self.wait(shard(1), sem(1))
            push(shard(1), ("z", 7), 5)
        elif t == 2:
            self.wait(shard(5), sem(2))
            self.wait(shard(3), sem(3))
            push(w.at[xh, :, odd, k, over], "cross", 7)
            if c % 2 == 0:
                push(shard(5), ("z", 1), 6)
            else:
                push(shard(3), ("z", 7), 6)
        elif t == 3:
            self.wait(shard(6), sem(4))
            self.wait(shard(2), sem(5))
            self.wait(shard(4), sem(6))
            push(w.at[xh, :, even, k, over], "cross", 8)
            if kind in "QH":
                spread(xh, fetch, 9)
            else:
                push(w.at[xh, :, :, k, full], "core", 12)
        elif t == 4:
            self.wait(w.at[1 - xh, :, odd, k, theirs], sem(7))
            if halved:
                spread(1 - xh, theirs, 10, odd)
        elif t == 5:
            self.wait(w.at[1 - xh, :, even, k, theirs], sem(8))
            if kind == "C":
                push(w.at[1 - xh, :, :, k, full], "core", 13)
            else:
                spread(1 - xh, theirs, 11, even if halved else slice(None))
        elif t == 6:
            if kind in "QH":
                self.wait(w.at[xh, :, :, k, brought], sem(9))
                push(w.at[xh, :, :, k, full], "core", 12)
        elif t == 7:
            if halved:
                self.wait(w.at[xh, :, 0, k, brought], sem(10))
                self.wait(w.at[xh, :, 0, k, brought], sem(11))
            elif kind != "C":
                self.wait(w.at[xh, :, :, k, brought], sem(11))
            if kind != "C":
                push(w.at[1 - xh, :, :, k, full], "core", 13)
        else:
            self.wait(w.at[xh, :, :, k, full], sem(12))
            self.wait(w.at[xh, :, :, k, full], sem(13))

    def halo(self, src, dst, base, at, to, sign, sem):
        for i, (a, b) in enumerate(((1, 0), (0, 1), (1, 1))):
            rows = at[i + 1] - at[i]
            self.copy(
                src.at[pl.ds(base + at[i], rows)], dst.at[pl.ds(to + at[i], rows)],
                ("halo", sign * a, sign * b), sem,
            )


def kernel(
    x_in, gain1, gain2, qkv1, proj1, merge, qkv2, proj2, up_w, skip_w,
    m0, m1, m2, m3, m4, m5, m6, out,
    pack_x, to_win, pack_f, to_quad, to_own, pack_u, up_m,
    w, xe, snd_x, xw, qkv, fe, snd_f, qd, coarse, big, mixed, ue, snd_u, skipped, done, bias, send, recv, local,
):
    net = Net(w, send, recv)
    lat = lax.axis_index("lat")

    loads = []

    def load(src, dst):
        d = pltpu.make_async_copy(src, dst, local.at[len(loads)])
        d.start()
        loads.append(d)
        return d

    row = 0
    for ref in (qkv1, proj1, merge, qkv2, proj2, up_w, skip_w):
        rows, cols = ref.shape
        for b in range(cols // 512):
            load(ref.at[:, pl.ds(512 * b, 512)], w.at[net.xh, net.z // 2, net.z % 2, net.k, pl.ds(row, rows)])
            row += rows
    shards = list(loads)
    field = load(x_in, xe.at[:, pl.ds(0, 576)])
    order = [load(a, b) for a, b in zip((m0, m1, m2, m3, m4, m5, m6), (pack_x, to_win, pack_f, to_quad, to_own, pack_u, up_m))]
    for d in shards:
        d.wait()
    barrier = pltpu.get_barrier_semaphore()
    for name in net.dev:
        pl.semaphore_signal(barrier, inc=1, device_id=net.to(name), device_id_type=MESH)
    field.wait()
    order[0].wait()
    for g in range(2):
        snd_x[g] = dot(pack_x[...], xe[g, pl.ds(0, 576)]).astype(BF16)
    pl.semaphore_wait(barrier, len(net.dev))


    col = lax.broadcasted_iota(jnp.int32, (288, 144), 1)
    rowi = lax.broadcasted_iota(jnp.int32, (288, 144), 0)
    rowi = jnp.where(rowi >= 144, rowi - 144, rowi)
    low = lambda t: jnp.where(t >= 72, t - 72, t) >= 36
    apart = jnp.logical_xor(low(rowi), low(col))
    last = (lat == 7).astype(F32)
    bias[...] = jnp.where(apart, -1e30, 0.0) * last
    left = (lax.broadcasted_iota(jnp.int32, (144, 128), 1) < 64).astype(F32)
    left16 = left.astype(BF16)
    right16 = (1.0 - left).astype(BF16)
    ones = jnp.ones((144, 128), BF16)
    late, leaving = [], []

    def ready(i):
        if i not in late:
            late.append(i)
            order[i].wait()

    def weight(at, rows):
        return w[:, :, :, :, pl.ds(at, rows), :].reshape(32 * rows, 512)

    def attend(src, at, rows, heads, masked, dst):
        scores = []
        for h in heads:
            q = src[rows, pl.ds(at[0] + 128 * h, 128)]
            keys = src[rows, pl.ds(at[1] + 128 * h, 128)]
            q = jnp.concatenate([q * left16, q * right16], axis=0)
            s = lax.dot_general(q, keys, (((1,), (1,)), ((), ())), preferred_element_type=F32)
            scores.append(s + bias[...] if masked else s)
        parts = [jnp.exp(s - jnp.max(s, axis=-1, keepdims=True)).astype(BF16) for s in scores]
        for h, p in zip(heads, parts):
            vals = src[rows, pl.ds(at[2] + 128 * h, 128)]
            o = dot(p, jnp.concatenate([vals, ones], axis=1))
            o = o[:, :128] / o[:, 128:]
            dst[rows, pl.ds(128 * h, 128)] = jnp.where(left > 0.5, o[:144], o[144:]).astype(BF16)

    field_at, first_at, term_at = (0, 112, 224, 272), (0, 112, 224, 272), (0, 48, 96, 144)

    def packx():
        for g in range(2):
            net.halo(snd_x.at[g], xe.at[g], 0, field_at, 576, -1, 140 + g)

    def win(g):
        ready(1)
        net.wait(xe.at[g, pl.ds(576, 272)], 140 + g)
        xw[g] = dot(to_win[...], xe[g]).astype(BF16)

    def qkv1_(g, b):
        def one(i, _):
            rows = pl.ds(pl.multiple_of(i * 288, 16), 288)
            o = dot(xw[g, rows], weight(QKV1 + 16 * b, 16))
            qkv[rows, pl.ds(512 * b, 512)] = (o * 0.125 if b == 0 else o).astype(BF16)
            return 0

        lax.fori_loop(0, 2, one, 0)

    def att(g, n):
        rows, inside = pl.ds(n * 144, 144), pl.ds(272 + n * 144, 144)
        attend(qkv, (0, 512, 1024), rows, (0, 1), n >= 2, mixed)
        attend(qkv, (0, 512, 1024), rows, (2, 3), n >= 2, mixed)
        branch = norm(dot(mixed[rows, pl.ds(0, 512)], weight(PROJ1, 16)), gain1[...]).astype(BF16)
        fe[g, inside] = (xw[g, rows].astype(F32) + branch.astype(F32)).astype(BF16)

    def packf(g):
        ready(2)
        snd_f[g] = dot(pack_f[...], fe[g, pl.ds(272, 576)]).astype(BF16)
        net.halo(snd_f.at[g], fe.at[g], 0, first_at, 0, -1, 142 + g)

    def bwd(g):
        net.halo(snd_f.at[g], fe.at[g], 272, first_at, 848, 1, 144 + g)

    def quads(g):
        ready(3)
        net.wait(fe.at[g, pl.ds(0, 272)], 142 + g)
        picked = dot(to_quad[...], fe[g, pl.ds(0, 848)]).astype(BF16)
        for q in range(4):
            qd[:, pl.ds(512 * q, 512)] = picked[144 * q : 144 * (q + 1)]

    def merge_(g, b):
        coarse[g, :, pl.ds(512 * b, 512)] = dot(qd[...], weight(MERGE + 64 * b, 64)).astype(BF16)

    def qkv2_(g, b):
        o = dot(coarse[g], weight(QKV2 + 32 * b, 32))
        big[:, pl.ds(512 * b, 512)] = (o * 0.125 if b < 2 else o).astype(BF16)

    def att2_(g, i):
        attend(big, (0, 1024, 2048), pl.ds(0, 144), (2 * i, 2 * i + 1), True, mixed)

    def proj2_(g):
        projected = jnp.concatenate([dot(mixed[pl.ds(0, 144)], weight(PROJ2 + 32 * b, 32)) for b in range(2)], axis=1)
        branch = norm(projected, gain2[...]).astype(BF16)
        coarse[g] = (coarse[g].astype(F32) + branch.astype(F32)).astype(BF16)

    def up(g):
        ready(5)
        term = dot(coarse[g], weight(UP, 32)).astype(BF16)
        ue[g, pl.ds(0, 144)] = term
        snd_u[g] = dot(pack_u[...], term).astype(BF16)
        net.halo(snd_u.at[g], ue.at[g], 0, term_at, 144, 1, 146 + g)

    def own(g):
        ready(4)
        net.wait(fe.at[g, pl.ds(848, 272)], 144 + g)
        xw[g] = dot(to_own[...], fe[g, pl.ds(272, 848)]).astype(BF16)

    def skip(g):
        def one(i, _):
            rows = pl.ds(pl.multiple_of(i * 288, 16), 288)
            skipped[g, rows] = dot(xw[g, rows], weight(SKIP, 16))
            return 0

        lax.fori_loop(0, 2, one, 0)

    def fin(g):
        ready(6)
        net.wait(ue.at[g, pl.ds(144, 144)], 146 + g)
        done[g] = (skipped[g] + dot(up_m[...], ue[g])).astype(BF16)
        leaving.append(pltpu.make_async_copy(done.at[g], out.at[g], local.at[24 + g]))
        leaving[-1].start()

    work = dict(
        packx=packx, win=win, qkv1_=qkv1_, att=att, packf=packf, bwd=bwd, quads=quads, merge=merge_,
        qkv2_=qkv2_, att2_=att2_, proj2_=proj2_, up=up, own=own, skip=skip, fin=fin,
    )
    for item in ORDER:
        if isinstance(item, int):
            net.step(item // 9, item % 9)
        else:
            work[item[0]](*item[1:])
    net.finish()
    for d in leaving:
        d.wait()


def body(field, gain1, qkv1, proj1, merge, gain2, qkv2, proj2, up_w, skip_w):
    constants = [jnp.asarray(m, BF16) for m in orders()]
    hbm, vmem = pl.BlockSpec(memory_space=pl.ANY), pl.BlockSpec(memory_space=pltpu.VMEM)
    v = lambda *shape: pltpu.VMEM(shape, BF16)
    out = pl.pallas_call(
        kernel,
        out_shape=jax.ShapeDtypeStruct((2, 576, 512), BF16),
        in_specs=[hbm, vmem, vmem] + [hbm] * 14,
        out_specs=hbm,
        scratch_shapes=[v(*m.shape) for m in constants] + [
            v(2, 4, 2, 2, ROWS, 512),
            v(2, 848, 512), v(2, 272, 512), v(2, 576, 512), v(576, 1536),
            v(2, 1120, 512), v(2, 544, 512), v(144, 2048), v(2, 144, 1024), v(144, 3072), v(576, 1024),
            v(2, 288, 512), v(2, 144, 512),
            pltpu.VMEM((2, 576, 512), F32), v(2, 576, 512), pltpu.VMEM((288, 144), F32),
            pltpu.SemaphoreType.DMA((200,)), pltpu.SemaphoreType.DMA((148,)), pltpu.SemaphoreType.DMA((26,)),
        ],
        compiler_params=pltpu.CompilerParams(collective_id=0, has_side_effects=True, vmem_limit_bytes=60 << 20),
    )(field.reshape(2, 576, 512), gain1.reshape(1, 512), gain2.reshape(1, 1024), qkv1, proj1, merge, qkv2, proj2, up_w, skip_w, *constants)
    return out.reshape(4, 12, 24, 512)


def solution(mesh):
    rows = P("lon", None)
    in_specs = (P(None, "lat", "lon", None), P(), rows, rows, rows, P(), rows, rows, rows, rows)
    return jax.shard_map(body, mesh=mesh, in_specs=in_specs, out_specs=P(None, "lat", "lon", None), check_vma=False)
```
